32 devices in a mesh: dp: 2 (over core), expert: 16 (over z, y, x).
Axes of the slice: x: 2, y: 2, z: 4, core: 2. Of those that a mesh axis runs over, the one named last changes fastest.
Arguments:
- tokens: bfloat16 [8192, 3584], P(('dp', 'expert')), may hold values from -6 to 6
- cotangent: bfloat16 [8192, 3584], P(('dp', 'expert')), may hold values from -6 to 6
- expert_ids: int32 [8192, 1], P(('dp', 'expert')), may hold values from 0 to 15; in each aligned block of 256 rows (0 to 255, 256 to 511, ...) at most 32 rows name the same one
- gate_probs: float32 [8192, 1], P(('dp', 'expert')), may hold values from 0.2 to 1
- w_gate: bfloat16 [16, 3584, 1024], P('expert', None, 'dp'), may hold values from -0.09375 to 0.09375
- w_up: bfloat16 [16, 3584, 1024], P('expert', None, 'dp'), may hold values from -0.09375 to 0.09375
- w_down: bfloat16 [16, 1024, 3584], P('expert', 'dp'), may hold values from -0.1875 to 0.1875
Outputs:
- grad_tokens: bfloat16 [8192, 3584], P(('dp', 'expert'))
- grad_gate: bfloat16 [16, 3584, 1024], P('expert', None, 'dp')
- grad_up: bfloat16 [16, 3584, 1024], P('expert', None, 'dp')
- grad_down: bfloat16 [16, 1024, 3584], P('expert', 'dp')
The draws below stay inside these ranges and needn't reach their ends.
Inputs may be any that keep to these rules, and one draw needn't show every extreme that they name: `expert_ids`: within the entries of one device's 256 tokens, no expert is named more than 32 times, and in some device one expert is named exactly 32 times. Each row names exactly one expert.
All inputs are finite; a program needn't handle non-finite values.
Results may differ from the reference program's by a relative error of at most 0.0065.
Values may be sent and summed in bfloat16 or wider, within the bound.
A program may use at most 192 MiB of HBM per device.

```python
import math
import jax
import jax.numpy as jnp
import numpy as np
from jax import lax

D = 3584
F = 1024
TOPK = 1
TOK_DEV = 256
EXPERTS = 16
TOKENS = 8192
CAP = 32
N_DP = 2
N_EXPERT = 16


def shard_levels(rng, shape, split, least, high):
    def one(axis_at, blocks):
        steps = jax.random.uniform(jax.random.fold_in(jax.random.fold_in(rng, 6), axis_at), (blocks,), jnp.float32, least / len(split), high / len(split))
        return jnp.repeat(jnp.exp(steps), shape[axis_at] // blocks).reshape((-1,) + (1,) * (len(shape) - axis_at - 1))

    factor_of = one(*split[0])
    for cut in split[1:]:
        factor_of = factor_of * one(*cut)
    return factor_of


def deal_out(own_key, own, number, rows, number_of, top, most, slope):
    sequence = jax.random.permutation(own_key, number_of)
    crowded, usual = load_shares(number_of, rows * top, most, slope, True), load_shares(number_of, rows * top, most, slope, False)
    places = jnp.arange(number_of)

    def named(sizes, turn):
        used = int((sizes > 0).sum())
        fixed = max(1, used // 4)
        passed = fixed + (places - fixed + turn * (used - fixed)) % max(1, number_of - fixed)
        return jnp.zeros((number_of,), jnp.int32).at[sequence[jnp.where(places < fixed, places, passed)]].set(jnp.asarray(sizes, jnp.int32))

    sizes = jnp.where(number % 4 == 0, named(crowded, number // 4), named(usual, number - number // 4 - 1))
    mixed = jax.random.permutation(jax.random.fold_in(own, 3), number_of)
    donor, receiver = mixed[0:number_of // 2 * 2:2], mixed[1:number_of // 2 * 2:2]
    room = jnp.minimum(sizes[donor] - 1, most - sizes[receiver]) // 2
    room = jnp.where((donor == sequence[0]) | (receiver == sequence[0]) | (sizes[receiver] == 0), 0, jnp.maximum(room, 0))
    passed = jax.random.randint(jax.random.fold_in(own, 4), (number_of // 2,), 0, 1 << 20) % (room + 1)
    sizes = sizes.at[donor].add(-passed).at[receiver].add(passed)
    labels = jnp.searchsorted(jnp.cumsum(sizes), jnp.arange(rows * top), side="right").astype(jnp.int32)
    grid = labels.reshape(top, rows).T
    grid = grid[jax.random.permutation(jax.random.fold_in(own, 1), rows)]
    turn = jax.random.randint(jax.random.fold_in(own, 2), (rows, 1), 0, top)
    return jnp.take_along_axis(grid, (jnp.arange(top)[None, :] + turn) % top, axis=1)


def load_shares(count, total, bound, slope, full):
    portions = [(1 << 20) // math.isqrt(rank ** slope) + 1 for rank in range(1, count + 1)]
    largest = bound if full else min(bound, max(-(-total // count), total * portions[0] // sum(portions)))
    least = 1 if total - largest >= count - 1 else 0
    holding, spare = [largest] + [least] * (count - 1), total - largest - least * (count - 1)
    while spare > 0:
        candidates = [i for i in range(1, count) if holding[i] < largest] or [i for i in range(1, count) if holding[i] < bound]
        pool, left = sum([portions[i] for i in candidates]), spare
        for i in candidates:
            extra = min(bound - holding[i], max(1, left * portions[i] // pool), spare)
            holding[i] = holding[i] + extra
            spare = spare - extra
    return np.array(holding)


def noise(stream_key, dims, scale, reach, pieces=(), held_as=jnp.bfloat16):
    result = jax.random.normal(stream_key, dims, jnp.float32) * scale
    if len(pieces) > 0:
        result = shard_levels(stream_key, dims, pieces, -0.22, 0.18) * result
    return jnp.clip(result, min=-reach, max=reach).astype(held_as)


def setup_inputs(seed: int = 0) -> dict:
    seeds = jax.random.split(jax.random.key(seed), 8)
    tokens = noise(seeds[0], (TOKENS, D), 1.0, 6.0, ((0, 32),))
    cotangent = noise(seeds[1], (TOKENS, D), 1.0, 6.0, ((0, 32),))
    expert_ids_keys = jax.random.split(jax.random.fold_in(seeds[2], 1), TOKENS // TOK_DEV)
    expert_ids_turns = jax.random.permutation(jax.random.fold_in(seeds[2], 3), TOKENS // TOK_DEV)
    expert_ids = jax.vmap(lambda own, number: deal_out(jax.random.fold_in(seeds[2], 2), own, number, TOK_DEV, EXPERTS, TOPK, CAP, 2))(expert_ids_keys, expert_ids_turns).reshape((TOKENS, TOPK))
    gate_probs = jnp.clip(0.2 + 0.8 * jax.random.uniform(seeds[3], (TOKENS, TOPK), jnp.float32) ** shard_levels(seeds[3], (TOKENS, TOPK), ((0, 32),), -0.2, 0.2), 0.2, 1.0)
    w_gate = noise(seeds[4], (EXPERTS, D, F), D ** -0.5, 0.09375, ((0, 16), (2, 2)))
    w_up = noise(seeds[5], (EXPERTS, D, F), D ** -0.5, 0.09375, ((0, 16), (2, 2)))
    w_down = noise(seeds[6], (EXPERTS, F, D), F ** -0.5, 0.1875, ((0, 16), (1, 2)))
    return {"tokens": tokens, "cotangent": cotangent, "expert_ids": expert_ids, "gate_probs": gate_probs, "w_gate": w_gate, "w_up": w_up, "w_down": w_down}


def expert_pass(rows_x, rows_cot, gate_w, up_w, down_w):
    gate_pre = jnp.dot(rows_x, gate_w, preferred_element_type=jnp.float32)
    up_pre = jnp.dot(rows_x, up_w, preferred_element_type=jnp.float32)
    sigmoid_gate = jax.nn.sigmoid(gate_pre)
    swish_gate = gate_pre * sigmoid_gate
    hidden = (swish_gate * up_pre).astype(jnp.bfloat16)
    d_hidden = lax.dot_general(rows_cot, down_w, (((1,), (1,)), ((), ())), preferred_element_type=jnp.float32)
    d_gate = (d_hidden * up_pre * sigmoid_gate * (1.0 + gate_pre * (1.0 - sigmoid_gate))).astype(jnp.bfloat16)
    d_up = (d_hidden * swish_gate).astype(jnp.bfloat16)
    grad_down = lax.dot_general(hidden, rows_cot, (((0,), (0,)), ((), ())), preferred_element_type=jnp.float32)
    grad_gate = lax.dot_general(rows_x, d_gate, (((0,), (0,)), ((), ())), preferred_element_type=jnp.float32)
    grad_up = lax.dot_general(rows_x, d_up, (((0,), (0,)), ((), ())), preferred_element_type=jnp.float32)
    return grad_gate, grad_up, grad_down, d_gate, d_up


def reference(tokens, cotangent, expert_ids, gate_probs, w_gate, w_up, w_down):
    copies = TOKENS * TOPK
    sources = N_DP * N_EXPERT
    flat_ids = expert_ids.reshape(copies).astype(jnp.int32)
    token_of = jnp.arange(copies, dtype=jnp.int32) // TOPK
    source_of = token_of // TOK_DEV
    onehot = (flat_ids[:, None] == jnp.arange(EXPERTS, dtype=jnp.int32)[None, :]).astype(jnp.int32)
    blocked = onehot.reshape(sources, TOK_DEV * TOPK, EXPERTS)
    before = (jnp.cumsum(blocked, axis=1) - blocked).reshape(copies, EXPERTS)
    slot_rank = jnp.sum(before * onehot, axis=1).astype(jnp.int32)
    position = (source_of * CAP + slot_rank).astype(jnp.int32)
    slot_table = jnp.full((EXPERTS, sources * CAP), copies, jnp.int32)
    slot_table = slot_table.at[flat_ids, position].set(jnp.arange(copies, dtype=jnp.int32))
    copy_rows = jnp.take(tokens, token_of, axis=0)
    copy_cot = (gate_probs.reshape(copies, 1) * jnp.take(cotangent, token_of, axis=0).astype(jnp.float32)).astype(jnp.bfloat16)
    block_width = F // N_DP

    def one_expert(operands):
        index_row, gate_w, up_w, down_w = operands
        rows_x = jnp.take(copy_rows, index_row, axis=0, mode="fill", fill_value=0)
        rows_cot = jnp.take(copy_cot, index_row, axis=0, mode="fill", fill_value=0)
        grad_gate, grad_up, grad_down, d_gate, d_up = expert_pass(rows_x, rows_cot, gate_w, up_w, down_w)
        summed = jnp.zeros(rows_x.shape, jnp.float32)
        for block_index in range(N_DP):
            lower_edge = block_index * block_width
            upper_edge = lower_edge + block_width
            block_part = lax.dot_general(d_gate[:, lower_edge:upper_edge], gate_w[:, lower_edge:upper_edge], (((1,), (1,)), ((), ())), preferred_element_type=jnp.float32)
            block_part = block_part + lax.dot_general(d_up[:, lower_edge:upper_edge], up_w[:, lower_edge:upper_edge], (((1,), (1,)), ((), ())), preferred_element_type=jnp.float32)
            summed = summed + lax.optimization_barrier(block_part.astype(jnp.bfloat16)).astype(jnp.float32)
        return grad_gate.astype(jnp.bfloat16), grad_up.astype(jnp.bfloat16), grad_down.astype(jnp.bfloat16), summed.astype(jnp.bfloat16)

    grad_gate, grad_up, grad_down, copy_back = lax.map(one_expert, (slot_table, w_gate, w_up, w_down))
    copy_grad = copy_back[flat_ids, position]
    grad_tokens = jnp.sum(copy_grad.reshape(TOKENS, TOPK, D).astype(jnp.float32), axis=1).astype(jnp.bfloat16)
    return grad_tokens, grad_gate, grad_up, grad_down
```

```python
import jax
import jax.numpy as jnp
from jax import lax
from jax.sharding import PartitionSpec as P


def front_rows(rows_x, rows_cot, gate_w, up_w, down_w):
    gate_pre = jnp.dot(rows_x, gate_w, preferred_element_type=jnp.float32)
    up_pre = jnp.dot(rows_x, up_w, preferred_element_type=jnp.float32)
    sigmoid_gate = jax.nn.sigmoid(gate_pre)
    swish_gate = gate_pre * sigmoid_gate
    hidden = (swish_gate * up_pre).astype(jnp.bfloat16)
    d_hidden = lax.dot_general(
        rows_cot, down_w, (((1,), (1,)), ((), ())), preferred_element_type=jnp.float32
    )
    d_gate = (d_hidden * up_pre * sigmoid_gate * (1.0 + gate_pre * (1.0 - sigmoid_gate))).astype(
        jnp.bfloat16
    )
    d_up = (d_hidden * swish_gate).astype(jnp.bfloat16)
    dx_part = lax.dot_general(
        d_gate, gate_w, (((1,), (1,)), ((), ())), preferred_element_type=jnp.float32
    )
    dx_part = dx_part + lax.dot_general(
        d_up, up_w, (((1,), (1,)), ((), ())), preferred_element_type=jnp.float32
    )
    return (hidden, d_gate, d_up, dx_part.astype(jnp.bfloat16))


def weight_sums(rows_x, rows_cot, hidden, d_gate, d_up):
    grad_gate = lax.dot_general(
        rows_x, d_gate, (((0,), (0,)), ((), ())), preferred_element_type=jnp.float32
    )
    grad_up = lax.dot_general(
        rows_x, d_up, (((0,), (0,)), ((), ())), preferred_element_type=jnp.float32
    )
    grad_down = lax.dot_general(
        hidden, rows_cot, (((0,), (0,)), ((), ())), preferred_element_type=jnp.float32
    )
    return (grad_gate, grad_up, grad_down)


def local(tokens, cotangent, expert_ids, gate_probs, w_gate, w_up, w_down):
    owners = lax.axis_size("expert")
    groups = lax.axis_size("dp")
    tok_rows = tokens.shape[0]
    model_width = tokens.shape[1]
    fanout = expert_ids.shape[1]
    capacity = max(2, 2 * tok_rows * fanout // owners)
    copies = tok_rows * fanout
    flat_ids = expert_ids.reshape(copies)
    onehot = (flat_ids[:, None] == jnp.arange(owners, dtype=jnp.int32)[None, :]).astype(jnp.int32)
    before = jnp.cumsum(onehot, axis=0) - onehot
    slot_rank = jnp.sum(before * onehot, axis=1)
    position = flat_ids * capacity + slot_rank
    copy_rows = tokens[:, None, :].reshape(copies, model_width)
    copy_tok_cot = cotangent[:, None, :].reshape(copies, model_width)
    copy_cots = (gate_probs * copy_tok_cot.astype(jnp.float32)).astype(jnp.bfloat16)
    placing = (jnp.arange(owners * capacity, dtype=jnp.int32)[:, None] == position[None, :]).astype(
        jnp.bfloat16
    )
    sent_rows = (
        jnp.dot(placing, copy_rows, preferred_element_type=jnp.float32)
        .astype(jnp.bfloat16)
        .reshape(owners, capacity, model_width)
    )
    sent_cots = (
        jnp.dot(placing, copy_cots, preferred_element_type=jnp.float32)
        .astype(jnp.bfloat16)
        .reshape(owners, capacity, model_width)
    )
    came_rows = lax.all_to_all(sent_rows, "expert", split_axis=0, concat_axis=0, tiled=True)
    came_cots = lax.all_to_all(sent_cots, "expert", split_axis=0, concat_axis=0, tiled=True)
    got_rows = lax.all_gather(came_rows, "dp", axis=0, tiled=True)
    got_cots = lax.all_gather(came_cots, "dp", axis=0, tiled=True)
    slots_all = owners * groups * capacity
    rows_x = got_rows.reshape(slots_all, model_width)
    rows_cot = got_cots.reshape(slots_all, model_width)
    hidden, d_gate, d_up, dx_part = front_rows(rows_x, rows_cot, w_gate[0], w_up[0], w_down[0])
    summed = lax.psum_scatter(
        dx_part.reshape(groups * owners, capacity, model_width),
        "dp",
        scatter_dimension=0,
        tiled=True,
    )
    returned = lax.all_to_all(summed, "expert", split_axis=0, concat_axis=0, tiled=True)
    grad_gate, grad_up, grad_down = weight_sums(rows_x, rows_cot, hidden, d_gate, d_up)
    copy_grad = lax.dot_general(
        placing,
        returned.reshape(owners * capacity, model_width),
        (((0,), (0,)), ((), ())),
        preferred_element_type=jnp.float32,
    )
    grad_tokens = jnp.sum(copy_grad.reshape(tok_rows, fanout, model_width), axis=1).astype(
        jnp.bfloat16
    )
    return (
        grad_tokens,
        grad_gate.astype(jnp.bfloat16)[None],
        grad_up.astype(jnp.bfloat16)[None],
        grad_down.astype(jnp.bfloat16)[None],
    )


def solution(mesh):
    return jax.shard_map(
        local,
        mesh=mesh,
        in_specs=(
            P(("dp", "expert"), None),
            P(("dp", "expert"), None),
            P(("dp", "expert"), None),
            P(("dp", "expert"), None),
            P("expert", None, "dp"),
            P("expert", None, "dp"),
            P("expert", "dp", None),
        ),
        out_specs=(
            P(("dp", "expert"), None),
            P("expert", None, "dp"),
            P("expert", None, "dp"),
            P("expert", "dp", None),
        ),
        check_vma=False,
    )
```

```python
import functools

import jax
import jax.numpy as jnp
from jax import lax
from jax.experimental import pallas as pl
from jax.experimental.pallas import tpu as pltpu
from jax.sharding import PartitionSpec as P

MESH = pl.DeviceIdType.MESH
NT = (((1,), (1,)), ((), ()))
TN = (((0,), (0,)), ((), ()))


def hop_of(step, owners):
    return (step % 2) * (owners // 2) + step // 2


def layer_kernel(
    owners,
    capacity,
    tile_steps,
    sx,
    sc,
    w_gate,
    w_up,
    w_down,
    ret,
    out_gate,
    out_up,
    out_down,
    gx,
    gc,
    wg,
    wu,
    wd,
    dx,
    pin,
    hidden,
    d_gate,
    d_up,
    local_sem,
    x_send,
    x_recv,
    c_send,
    c_recv,
    fx_send,
    fx_recv,
    fc_send,
    fc_recv,
    p_send,
    p_recv,
    r_send,
    r_recv,
):
    me = lax.axis_index("expert")
    other = {"dp": 1 - lax.axis_index("dp")}
    model_width = gx.shape[1]
    hidden_width = wg.shape[1]
    tiles = owners // tile_steps
    tile_rows = tile_steps * 2 * capacity
    f32 = jnp.float32

    def ahead(step):
        return {"expert": (me + hop_of(step, owners)) % owners}

    def behind(step):
        return {"expert": (me + owners - hop_of(step, owners)) % owners}

    def sent(ref, step):
        return ref.at[pl.ds(pl.multiple_of(step * capacity, 16), capacity), :]

    def mine(ref, step):
        return ref.at[pl.ds(pl.multiple_of(step * 2 * capacity, 16), capacity), :]

    def theirs(ref, step):
        return ref.at[pl.ds(pl.multiple_of(step * 2 * capacity + capacity, 16), capacity), :]

    def remote(src, dst, send, recv, step, device):
        return pltpu.make_async_remote_copy(
            src_ref=src,
            dst_ref=dst,
            send_sem=send.at[step],
            recv_sem=recv.at[step],
            device_id=device,
            device_id_type=MESH,
        )

    def x_copy(step):
        return remote(sent(sx, step), mine(gx, step), x_send, x_recv, step, ahead(step))

    def c_copy(step):
        return remote(sent(sc, step), mine(gc, step), c_send, c_recv, step, ahead(step))

    def fx_copy(step):
        return remote(mine(gx, step), theirs(gx, step), fx_send, fx_recv, step, other)

    def fc_copy(step):
        return remote(mine(gc, step), theirs(gc, step), fc_send, fc_recv, step, other)

    def p_copy(step):
        return remote(theirs(dx, step), sent(pin, step), p_send, p_recv, step, other)

    def r_copy(step):
        return remote(mine(dx, step), sent(ret, step), r_send, r_recv, step, behind(step))

    barrier = pltpu.get_barrier_semaphore()
    pl.semaphore_signal(barrier, inc=1, device_id=other, device_id_type=MESH)

    @pl.loop(1, owners)
    def _(hop):
        pl.semaphore_signal(
            barrier, inc=1, device_id={"expert": (me + hop) % owners}, device_id_type=MESH
        )

    pl.semaphore_wait(barrier, owners)

    @pl.loop(1, owners)
    def _(step):
        x_copy(step).start()
        c_copy(step).start()

    own = [
        pltpu.make_async_copy(sent(sx, 0), mine(gx, 0), local_sem.at[0]),
        pltpu.make_async_copy(sent(sc, 0), mine(gc, 0), local_sem.at[1]),
        pltpu.make_async_copy(w_gate, wg, local_sem.at[2]),
        pltpu.make_async_copy(w_up, wu, local_sem.at[3]),
        pltpu.make_async_copy(w_down, wd, local_sem.at[4]),
    ]
    for copy in own:
        copy.start()
    for copy in own:
        copy.wait()
    fx_copy(0).start()
    fc_copy(0).start()

    column = 256
    width = next(w for w in (512, 256, 128) if model_width % w == 0)

    @pl.loop(0, tiles)
    def _(tile):
        first = tile * tile_steps

        @pl.loop(jnp.maximum(first, 1), first + tile_steps)
        def _(step):
            x_copy(step).wait_recv()
            fx_copy(step).start()
            c_copy(step).wait_recv()
            fc_copy(step).start()

        @pl.loop(first, first + tile_steps)
        def _(step):
            fx_copy(step).wait_recv()
            fc_copy(step).wait_recv()

        rows = pl.ds(pl.multiple_of(tile * tile_rows, 16), tile_rows)

        @pl.loop(0, hidden_width // column)
        def _(part):
            cols = pl.ds(pl.multiple_of(part * column, 128), column)
            gate_pre = jnp.dot(gx[rows, :], wg[:, cols], preferred_element_type=f32)
            up_pre = jnp.dot(gx[rows, :], wu[:, cols], preferred_element_type=f32)
            d_hidden = lax.dot_general(gc[rows, :], wd[cols, :], NT, preferred_element_type=f32)
            sigmoid_gate = jax.nn.sigmoid(gate_pre)
            swish_gate = gate_pre * sigmoid_gate
            hidden[rows, cols] = (swish_gate * up_pre).astype(jnp.bfloat16)
            d_gate[rows, cols] = (
                d_hidden * up_pre * sigmoid_gate * (1.0 + gate_pre * (1.0 - sigmoid_gate))
            ).astype(jnp.bfloat16)
            d_up[rows, cols] = (d_hidden * swish_gate).astype(jnp.bfloat16)

        @pl.loop(0, model_width // width)
        def _(part):
            cols = pl.ds(pl.multiple_of(part * width, 128), width)
            total = lax.dot_general(d_gate[rows, :], wg[cols, :], NT, preferred_element_type=f32)
            total += lax.dot_general(d_up[rows, :], wu[cols, :], NT, preferred_element_type=f32)
            dx[rows, cols] = total.astype(jnp.bfloat16)

        @pl.loop(first, first + tile_steps)
        def _(step):
            p_copy(step).start()

        @pl.loop(first, first + tile_steps)
        def _(step):
            p_copy(step).wait_recv()
            held = mine(dx, step)
            held[...] = (held[...].astype(f32) + sent(pin, step)[...].astype(f32)).astype(
                jnp.bfloat16
            )

            @pl.when(step > 0)
            def _():
                r_copy(step).start()

    back = pltpu.make_async_copy(mine(dx, 0), sent(ret, 0), local_sem.at[0])
    back.start()

    @pl.loop(0, model_width // width)
    def _(part):
        cols = pl.ds(pl.multiple_of(part * width, 128), width)
        wg[cols, :] = lax.dot_general(
            gx[:, cols], d_gate[...], TN, preferred_element_type=f32
        ).astype(jnp.bfloat16)
        wu[cols, :] = lax.dot_general(
            gx[:, cols], d_up[...], TN, preferred_element_type=f32
        ).astype(jnp.bfloat16)
        wd[:, cols] = lax.dot_general(
            hidden[...], gc[:, cols], TN, preferred_element_type=f32
        ).astype(jnp.bfloat16)

    results = [
        pltpu.make_async_copy(wg, out_gate, local_sem.at[2]),
        pltpu.make_async_copy(wu, out_up, local_sem.at[3]),
        pltpu.make_async_copy(wd, out_down, local_sem.at[4]),
    ]
    for copy in results:
        copy.start()

    @pl.loop(0, owners)
    def _(step):
        fx_copy(step).wait_send()
        fc_copy(step).wait_send()
        p_copy(step).wait_send()

    @pl.loop(1, owners)
    def _(step):
        x_copy(step).wait_send()
        c_copy(step).wait_send()
        r_copy(step).wait_send()
        r_copy(step).wait_recv()

    back.wait()
    for copy in results:
        copy.wait()


def run_layer(sent_rows, sent_cots, gate_w, up_w, down_w, owners, capacity):
    model_width = sent_rows.shape[1]
    hidden_width = gate_w.shape[1]
    slots = owners * capacity
    bf16 = jnp.bfloat16
    anywhere = pl.BlockSpec(memory_space=pl.ANY)
    tile_steps = max(1, 128 // capacity)
    return pl.pallas_call(
        functools.partial(layer_kernel, owners, capacity, tile_steps),
        out_shape=(
            jax.ShapeDtypeStruct((slots, model_width), bf16),
            jax.ShapeDtypeStruct(gate_w.shape, bf16),
            jax.ShapeDtypeStruct(up_w.shape, bf16),
            jax.ShapeDtypeStruct(down_w.shape, bf16),
        ),
        in_specs=[anywhere] * 5,
        out_specs=[anywhere] * 4,
        scratch_shapes=[
            pltpu.VMEM((2 * slots, model_width), bf16),
            pltpu.VMEM((2 * slots, model_width), bf16),
            pltpu.VMEM(gate_w.shape, bf16),
            pltpu.VMEM(up_w.shape, bf16),
            pltpu.VMEM(down_w.shape, bf16),
            pltpu.VMEM((2 * slots, model_width), bf16),
            pltpu.VMEM((slots, model_width), bf16),
            pltpu.VMEM((2 * slots, hidden_width), bf16),
            pltpu.VMEM((2 * slots, hidden_width), bf16),
            pltpu.VMEM((2 * slots, hidden_width), bf16),
            pltpu.SemaphoreType.DMA((5,)),
        ]
        + [pltpu.SemaphoreType.DMA((owners,))] * 12,
        compiler_params=pltpu.CompilerParams(
            collective_id=0, has_side_effects=True, vmem_limit_bytes=60 * 1024 * 1024
        ),
    )(sent_rows, sent_cots, gate_w, up_w, down_w)


def front_rows(rows_x, rows_cot, gate_w, up_w, down_w):
    gate_pre = jnp.dot(rows_x, gate_w, preferred_element_type=jnp.float32)
    up_pre = jnp.dot(rows_x, up_w, preferred_element_type=jnp.float32)
    sigmoid_gate = jax.nn.sigmoid(gate_pre)
    swish_gate = gate_pre * sigmoid_gate
    hidden = (swish_gate * up_pre).astype(jnp.bfloat16)
    d_hidden = lax.dot_general(
        rows_cot, down_w, (((1,), (1,)), ((), ())), preferred_element_type=jnp.float32
    )
    d_gate = (d_hidden * up_pre * sigmoid_gate * (1.0 + gate_pre * (1.0 - sigmoid_gate))).astype(
        jnp.bfloat16
    )
    d_up = (d_hidden * swish_gate).astype(jnp.bfloat16)
    dx_part = lax.dot_general(
        d_gate, gate_w, (((1,), (1,)), ((), ())), preferred_element_type=jnp.float32
    )
    dx_part = dx_part + lax.dot_general(
        d_up, up_w, (((1,), (1,)), ((), ())), preferred_element_type=jnp.float32
    )
    return (hidden, d_gate, d_up, dx_part.astype(jnp.bfloat16))


def weight_sums(rows_x, rows_cot, hidden, d_gate, d_up):
    grad_gate = lax.dot_general(
        rows_x, d_gate, (((0,), (0,)), ((), ())), preferred_element_type=jnp.float32
    )
    grad_up = lax.dot_general(
        rows_x, d_up, (((0,), (0,)), ((), ())), preferred_element_type=jnp.float32
    )
    grad_down = lax.dot_general(
        hidden, rows_cot, (((0,), (0,)), ((), ())), preferred_element_type=jnp.float32
    )
    return (grad_gate, grad_up, grad_down)


def run_whole(sent_rows, sent_cots, gate_w, up_w, down_w, owners, groups, capacity):
    model_width = sent_rows.shape[1]

    def across(rows):
        blocks = rows.reshape(owners, capacity, model_width)
        came = lax.all_to_all(blocks, "expert", split_axis=0, concat_axis=0, tiled=True)
        return lax.all_gather(came, "dp", axis=0, tiled=True).reshape(-1, model_width)

    rows_x, rows_cot = across(sent_rows), across(sent_cots)
    hidden, d_gate, d_up, dx_part = front_rows(rows_x, rows_cot, gate_w, up_w, down_w)
    summed = lax.psum_scatter(
        dx_part.reshape(groups * owners, capacity, model_width),
        "dp",
        scatter_dimension=0,
        tiled=True,
    )
    returned = lax.all_to_all(summed, "expert", split_axis=0, concat_axis=0, tiled=True)
    sums = weight_sums(rows_x, rows_cot, hidden, d_gate, d_up)
    return (returned.reshape(-1, model_width), *sums)


def local(tokens, cotangent, expert_ids, gate_probs, w_gate, w_up, w_down):
    owners = lax.axis_size("expert")
    groups = lax.axis_size("dp")
    tok_rows = tokens.shape[0]
    model_width = tokens.shape[1]
    fanout = expert_ids.shape[1]
    capacity = max(2, 2 * tok_rows * fanout // owners)
    copies = tok_rows * fanout
    in_kernel = groups == 2 and capacity % 16 == 0 and owners % max(1, 128 // capacity) == 0
    flat_ids = expert_ids.reshape(copies)
    targets = jnp.arange(owners, dtype=jnp.int32)
    if in_kernel:
        targets = (lax.axis_index("expert") + hop_of(targets, owners)) % owners
    onehot = (flat_ids[:, None] == targets[None, :]).astype(jnp.int32)
    order = jnp.arange(copies, dtype=jnp.int32)
    earlier = (order[None, :] < order[:, None]).astype(jnp.float32)
    before = lax.dot(
        earlier, onehot.astype(jnp.float32), precision=lax.Precision.HIGHEST
    ).astype(jnp.int32)
    slot_rank = jnp.sum(before * onehot, axis=1)
    block = jnp.sum(onehot * jnp.arange(owners, dtype=jnp.int32)[None, :], axis=1)
    position = block * capacity + slot_rank
    copy_rows = tokens[:, None, :].reshape(copies, model_width)
    copy_tok_cot = cotangent[:, None, :].reshape(copies, model_width)
    copy_cots = (gate_probs * copy_tok_cot.astype(jnp.float32)).astype(jnp.bfloat16)
    placing = (jnp.arange(owners * capacity, dtype=jnp.int32)[:, None] == position[None, :]).astype(
        jnp.bfloat16
    )
    sent_rows = jnp.dot(placing, copy_rows, preferred_element_type=jnp.float32).astype(jnp.bfloat16)
    sent_cots = jnp.dot(placing, copy_cots, preferred_element_type=jnp.float32).astype(jnp.bfloat16)
    if in_kernel:
        returned, grad_gate, grad_up, grad_down = run_layer(
            sent_rows, sent_cots, w_gate[0], w_up[0], w_down[0], owners, capacity
        )
    else:
        returned, grad_gate, grad_up, grad_down = run_whole(
            sent_rows, sent_cots, w_gate[0], w_up[0], w_down[0], owners, groups, capacity
        )
    copy_grad = lax.dot_general(placing, returned, TN, preferred_element_type=jnp.float32)
    grad_tokens = jnp.sum(copy_grad.reshape(tok_rows, fanout, model_width), axis=1).astype(
        jnp.bfloat16
    )
    return (
        grad_tokens,
        grad_gate.astype(jnp.bfloat16)[None],
        grad_up.astype(jnp.bfloat16)[None],
        grad_down.astype(jnp.bfloat16)[None],
    )


def solution(mesh):
    return jax.shard_map(
        local,
        mesh=mesh,
        in_specs=(
            P(("dp", "expert"), None),
            P(("dp", "expert"), None),
            P(("dp", "expert"), None),
            P(("dp", "expert"), None),
            P("expert", None, "dp"),
            P("expert", None, "dp"),
            P("expert", "dp", None),
        ),
        out_specs=(
            P(("dp", "expert"), None),
            P("expert", None, "dp"),
            P("expert", None, "dp"),
            P("expert", "dp", None),
        ),
        check_vma=False,
    )
```

```python
import functools

import jax
import jax.numpy as jnp
from jax import lax
from jax.experimental import pallas as pl
from jax.experimental.pallas import tpu as pltpu
from jax.sharding import PartitionSpec as P

MESH = pl.DeviceIdType.MESH
NT = (((1,), (1,)), ((), ()))
TN = (((0,), (0,)), ((), ()))


def hop_of(step, owners):
    return (step % 2) * (owners // 2) + step // 2


def layer_kernel(
    owners,
    capacity,
    tile_steps,
    placing,
    rows_in,
    cots_in,
    w_gate,
    w_up,
    w_down,
    ret,
    out_gate,
    out_up,
    out_down,
    sx,
    sc,
    gx,
    gc,
    wg,
    wu,
    wd,
    dx,
    pin,
    hidden,
    d_gate,
    d_up,
    local_sem,
    x_send,
    x_recv,
    c_send,
    c_recv,
    fx_send,
    fx_recv,
    fc_send,
    fc_recv,
    p_send,
    p_recv,
    r_send,
    r_recv,
):
    me = lax.axis_index("expert")
    other = {"dp": 1 - lax.axis_index("dp")}
    model_width = gx.shape[1]
    hidden_width = wg.shape[1]
    tiles = owners // tile_steps
    tile_rows = tile_steps * 2 * capacity
    f32 = jnp.float32

    def ahead(step):
        return {"expert": (me + hop_of(step, owners)) % owners}

    def behind(step):
        return {"expert": (me + owners - hop_of(step, owners)) % owners}

    def sent(ref, step):
        return ref.at[pl.ds(pl.multiple_of(step * capacity, 16), capacity), :]

    def mine(ref, step):
        return ref.at[pl.ds(pl.multiple_of(step * 2 * capacity, 16), capacity), :]

    def theirs(ref, step):
        return ref.at[pl.ds(pl.multiple_of(step * 2 * capacity + capacity, 16), capacity), :]

    def remote(src, dst, send, recv, step, device):
        return pltpu.make_async_remote_copy(
            src_ref=src,
            dst_ref=dst,
            send_sem=send.at[step],
            recv_sem=recv.at[step],
            device_id=device,
            device_id_type=MESH,
        )

    def x_copy(step):
        return remote(sent(sx, step), mine(gx, step), x_send, x_recv, step, ahead(step))

    def c_copy(step):
        return remote(sent(sc, step), mine(gc, step), c_send, c_recv, step, ahead(step))

    def fx_copy(step):
        return remote(mine(gx, step), theirs(gx, step), fx_send, fx_recv, step, other)

    def fc_copy(step):
        return remote(mine(gc, step), theirs(gc, step), fc_send, fc_recv, step, other)

    def p_copy(step):
        return remote(theirs(dx, step), sent(pin, step), p_send, p_recv, step, other)

    def r_copy(step):
        return remote(mine(dx, step), sent(ret, step), r_send, r_recv, step, behind(step))

    barrier = pltpu.get_barrier_semaphore()
    pl.semaphore_signal(barrier, inc=1, device_id=other, device_id_type=MESH)

    @pl.loop(1, owners)
    def _(hop):
        pl.semaphore_signal(
            barrier, inc=1, device_id={"expert": (me + hop) % owners}, device_id_type=MESH
        )

    pl.semaphore_wait(barrier, owners)

    def place(step):
        block = pl.ds(pl.multiple_of(step * capacity, 16), capacity)
        chosen = placing[block, :]
        sx[block, :] = jnp.dot(chosen, rows_in[...], preferred_element_type=f32).astype(jnp.bfloat16)
        sc[block, :] = jnp.dot(chosen, cots_in[...], preferred_element_type=f32).astype(jnp.bfloat16)

    @pl.loop(1, owners)
    def _(step):
        place(step)
        x_copy(step).start()
        c_copy(step).start()

    place(0)
    own = [
        pltpu.make_async_copy(sent(sx, 0), mine(gx, 0), local_sem.at[0]),
        pltpu.make_async_copy(sent(sc, 0), mine(gc, 0), local_sem.at[1]),
        pltpu.make_async_copy(w_gate, wg, local_sem.at[2]),
        pltpu.make_async_copy(w_up, wu, local_sem.at[3]),
        pltpu.make_async_copy(w_down, wd, local_sem.at[4]),
    ]
    for copy in own:
        copy.start()
    for copy in own:
        copy.wait()
    fx_copy(0).start()
    fc_copy(0).start()

    column = 256
    width = next(w for w in (512, 256, 128) if model_width % w == 0)

    @pl.loop(0, tiles)
    def _(tile):
        first = tile * tile_steps

        @pl.loop(jnp.maximum(first, 1), first + tile_steps)
        def _(step):
            x_copy(step).wait_recv()
            fx_copy(step).start()
            c_copy(step).wait_recv()
            fc_copy(step).start()

        @pl.loop(first, first + tile_steps)
        def _(step):
            fx_copy(step).wait_recv()
            fc_copy(step).wait_recv()

        rows = pl.ds(pl.multiple_of(tile * tile_rows, 16), tile_rows)

        @pl.loop(0, hidden_width // column)
        def _(part):
            cols = pl.ds(pl.multiple_of(part * column, 128), column)
            gate_pre = jnp.dot(gx[rows, :], wg[:, cols], preferred_element_type=f32)
            up_pre = jnp.dot(gx[rows, :], wu[:, cols], preferred_element_type=f32)
            d_hidden = lax.dot_general(gc[rows, :], wd[cols, :], NT, preferred_element_type=f32)
            sigmoid_gate = jax.nn.sigmoid(gate_pre)
            swish_gate = gate_pre * sigmoid_gate
            hidden[rows, cols] = (swish_gate * up_pre).astype(jnp.bfloat16)
            d_gate[rows, cols] = (
                d_hidden * up_pre * sigmoid_gate * (1.0 + gate_pre * (1.0 - sigmoid_gate))
            ).astype(jnp.bfloat16)
            d_up[rows, cols] = (d_hidden * swish_gate).astype(jnp.bfloat16)

        @pl.loop(0, model_width // width)
        def _(part):
            cols = pl.ds(pl.multiple_of(part * width, 128), width)
            total = lax.dot_general(d_gate[rows, :], wg[cols, :], NT, preferred_element_type=f32)
            total += lax.dot_general(d_up[rows, :], wu[cols, :], NT, preferred_element_type=f32)
            dx[rows, cols] = total.astype(jnp.bfloat16)

        @pl.loop(first, first + tile_steps)
        def _(step):
            p_copy(step).start()

        @pl.loop(first, first + tile_steps)
        def _(step):
            p_copy(step).wait_recv()
            held = mine(dx, step)
            held[...] = (held[...].astype(f32) + sent(pin, step)[...].astype(f32)).astype(
                jnp.bfloat16
            )

            @pl.when(step > 0)
            def _():
                r_copy(step).start()

    back = pltpu.make_async_copy(mine(dx, 0), sent(ret, 0), local_sem.at[0])
    back.start()

    @pl.loop(0, model_width // width)
    def _(part):
        cols = pl.ds(pl.multiple_of(part * width, 128), width)
        wg[cols, :] = lax.dot_general(
            gx[:, cols], d_gate[...], TN, preferred_element_type=f32
        ).astype(jnp.bfloat16)
        wu[cols, :] = lax.dot_general(
            gx[:, cols], d_up[...], TN, preferred_element_type=f32
        ).astype(jnp.bfloat16)
        wd[:, cols] = lax.dot_general(
            hidden[...], gc[:, cols], TN, preferred_element_type=f32
        ).astype(jnp.bfloat16)

    results = [
        pltpu.make_async_copy(wg, out_gate, local_sem.at[2]),
        pltpu.make_async_copy(wu, out_up, local_sem.at[3]),
        pltpu.make_async_copy(wd, out_down, local_sem.at[4]),
    ]
    for copy in results:
        copy.start()

    @pl.loop(0, owners)
    def _(step):
        fx_copy(step).wait_send()
        fc_copy(step).wait_send()
        p_copy(step).wait_send()

    @pl.loop(1, owners)
    def _(step):
        x_copy(step).wait_send()
        c_copy(step).wait_send()
        r_copy(step).wait_send()
        r_copy(step).wait_recv()

    back.wait()
    for copy in results:
        copy.wait()


def run_layer(placing, copy_rows, copy_cots, gate_w, up_w, down_w, owners, capacity):
    model_width = copy_rows.shape[1]
    hidden_width = gate_w.shape[1]
    slots = owners * capacity
    bf16 = jnp.bfloat16
    anywhere = pl.BlockSpec(memory_space=pl.ANY)
    tile_steps = max(1, 128 // capacity)
    return pl.pallas_call(
        functools.partial(layer_kernel, owners, capacity, tile_steps),
        out_shape=(
            jax.ShapeDtypeStruct((slots, model_width), bf16),
            jax.ShapeDtypeStruct(gate_w.shape, bf16),
            jax.ShapeDtypeStruct(up_w.shape, bf16),
            jax.ShapeDtypeStruct(down_w.shape, bf16),
        ),
        in_specs=[pl.BlockSpec(memory_space=pltpu.VMEM)] * 3 + [anywhere] * 3,
        out_specs=[anywhere] * 4,
        scratch_shapes=[
            pltpu.VMEM((slots, model_width), bf16),
            pltpu.VMEM((slots, model_width), bf16),
            pltpu.VMEM((2 * slots, model_width), bf16),
            pltpu.VMEM((2 * slots, model_width), bf16),
            pltpu.VMEM(gate_w.shape, bf16),
            pltpu.VMEM(up_w.shape, bf16),
            pltpu.VMEM(down_w.shape, bf16),
            pltpu.VMEM((2 * slots, model_width), bf16),
            pltpu.VMEM((slots, model_width), bf16),
            pltpu.VMEM((2 * slots, hidden_width), bf16),
            pltpu.VMEM((2 * slots, hidden_width), bf16),
            pltpu.VMEM((2 * slots, hidden_width), bf16),
            pltpu.SemaphoreType.DMA((5,)),
        ]
        + [pltpu.SemaphoreType.DMA((owners,))] * 12,
        compiler_params=pltpu.CompilerParams(
            collective_id=0, has_side_effects=True, vmem_limit_bytes=60 * 1024 * 1024
        ),
    )(placing, copy_rows, copy_cots, gate_w, up_w, down_w)


def front_rows(rows_x, rows_cot, gate_w, up_w, down_w):
    gate_pre = jnp.dot(rows_x, gate_w, preferred_element_type=jnp.float32)
    up_pre = jnp.dot(rows_x, up_w, preferred_element_type=jnp.float32)
    sigmoid_gate = jax.nn.sigmoid(gate_pre)
    swish_gate = gate_pre * sigmoid_gate
    hidden = (swish_gate * up_pre).astype(jnp.bfloat16)
    d_hidden = lax.dot_general(
        rows_cot, down_w, (((1,), (1,)), ((), ())), preferred_element_type=jnp.float32
    )
    d_gate = (d_hidden * up_pre * sigmoid_gate * (1.0 + gate_pre * (1.0 - sigmoid_gate))).astype(
        jnp.bfloat16
    )
    d_up = (d_hidden * swish_gate).astype(jnp.bfloat16)
    dx_part = lax.dot_general(
        d_gate, gate_w, (((1,), (1,)), ((), ())), preferred_element_type=jnp.float32
    )
    dx_part = dx_part + lax.dot_general(
        d_up, up_w, (((1,), (1,)), ((), ())), preferred_element_type=jnp.float32
    )
    return (hidden, d_gate, d_up, dx_part.astype(jnp.bfloat16))


def weight_sums(rows_x, rows_cot, hidden, d_gate, d_up):
    grad_gate = lax.dot_general(
        rows_x, d_gate, (((0,), (0,)), ((), ())), preferred_element_type=jnp.float32
    )
    grad_up = lax.dot_general(
        rows_x, d_up, (((0,), (0,)), ((), ())), preferred_element_type=jnp.float32
    )
    grad_down = lax.dot_general(
        hidden, rows_cot, (((0,), (0,)), ((), ())), preferred_element_type=jnp.float32
    )
    return (grad_gate, grad_up, grad_down)


def run_whole(sent_rows, sent_cots, gate_w, up_w, down_w, owners, groups, capacity):
    model_width = sent_rows.shape[1]

    def across(rows):
        blocks = rows.reshape(owners, capacity, model_width)
        came = lax.all_to_all(blocks, "expert", split_axis=0, concat_axis=0, tiled=True)
        return lax.all_gather(came, "dp", axis=0, tiled=True).reshape(-1, model_width)

    rows_x, rows_cot = across(sent_rows), across(sent_cots)
    hidden, d_gate, d_up, dx_part = front_rows(rows_x, rows_cot, gate_w, up_w, down_w)
    summed = lax.psum_scatter(
        dx_part.reshape(groups * owners, capacity, model_width),
        "dp",
        scatter_dimension=0,
        tiled=True,
    )
    returned = lax.all_to_all(summed, "expert", split_axis=0, concat_axis=0, tiled=True)
    sums = weight_sums(rows_x, rows_cot, hidden, d_gate, d_up)
    return (returned.reshape(-1, model_width), *sums)


def local(tokens, cotangent, expert_ids, gate_probs, w_gate, w_up, w_down):
    owners = lax.axis_size("expert")
    groups = lax.axis_size("dp")
    tok_rows = tokens.shape[0]
    model_width = tokens.shape[1]
    fanout = expert_ids.shape[1]
    capacity = max(2, 2 * tok_rows * fanout // owners)
    copies = tok_rows * fanout
    in_kernel = groups == 2 and capacity % 16 == 0 and owners % max(1, 128 // capacity) == 0
    flat_ids = expert_ids.reshape(copies)
    targets = jnp.arange(owners, dtype=jnp.int32)
    if in_kernel:
        targets = (lax.axis_index("expert") + hop_of(targets, owners)) % owners
    onehot = (flat_ids[:, None] == targets[None, :]).astype(jnp.int32)
    order = jnp.arange(copies, dtype=jnp.int32)
    earlier = (order[None, :] < order[:, None]).astype(jnp.float32)
    before = lax.dot(
        earlier, onehot.astype(jnp.float32), precision=lax.Precision.HIGHEST
    ).astype(jnp.int32)
    slot_rank = jnp.sum(before * onehot, axis=1)
    block = jnp.sum(onehot * jnp.arange(owners, dtype=jnp.int32)[None, :], axis=1)
    position = block * capacity + slot_rank
    copy_rows = tokens[:, None, :].reshape(copies, model_width)
    copy_tok_cot = cotangent[:, None, :].reshape(copies, model_width)
    copy_cots = (gate_probs * copy_tok_cot.astype(jnp.float32)).astype(jnp.bfloat16)
    placing = (jnp.arange(owners * capacity, dtype=jnp.int32)[:, None] == position[None, :]).astype(
        jnp.bfloat16
    )
    if in_kernel:
        returned, grad_gate, grad_up, grad_down = run_layer(
            placing, copy_rows, copy_cots, w_gate[0], w_up[0], w_down[0], owners, capacity
        )
    else:
        sent_rows = jnp.dot(placing, copy_rows, preferred_element_type=jnp.float32).astype(jnp.bfloat16)
        sent_cots = jnp.dot(placing, copy_cots, preferred_element_type=jnp.float32).astype(jnp.bfloat16)
        returned, grad_gate, grad_up, grad_down = run_whole(
            sent_rows, sent_cots, w_gate[0], w_up[0], w_down[0], owners, groups, capacity
        )
    copy_grad = lax.dot_general(placing, returned, TN, preferred_element_type=jnp.float32)
    grad_tokens = jnp.sum(copy_grad.reshape(tok_rows, fanout, model_width), axis=1).astype(
        jnp.bfloat16
    )
    return (
        grad_tokens,
        grad_gate.astype(jnp.bfloat16)[None],
        grad_up.astype(jnp.bfloat16)[None],
        grad_down.astype(jnp.bfloat16)[None],
    )


def solution(mesh):
    return jax.shard_map(
        local,
        mesh=mesh,
        in_specs=(
            P(("dp", "expert"), None),
            P(("dp", "expert"), None),
            P(("dp", "expert"), None),
            P(("dp", "expert"), None),
            P("expert", None, "dp"),
            P("expert", None, "dp"),
            P("expert", "dp", None),
        ),
        out_specs=(
            P(("dp", "expert"), None),
            P("expert", None, "dp"),
            P("expert", None, "dp"),
            P("expert", "dp", None),
        ),
        check_vma=False,
    )
```

```python
import functools

import jax
import jax.numpy as jnp
from jax import lax
from jax.experimental import pallas as pl
from jax.experimental.pallas import tpu as pltpu
from jax.sharding import PartitionSpec as P

MESH = pl.DeviceIdType.MESH
NT = (((1,), (1,)), ((), ()))
TN = (((0,), (0,)), ((), ()))


def hop_of(step, owners):
    return (step % 2) * (owners // 2) + step // 2


def layer_kernel(
    owners,
    capacity,
    tile_steps,
    placing,
    slot_probs,
    rows_in,
    cots_in,
    w_gate,
    w_up,
    w_down,
    ret,
    out_gate,
    out_up,
    out_down,
    sx,
    sc,
    gx,
    gc,
    wg,
    wu,
    wd,
    dx,
    pin,
    hidden,
    d_gate,
    d_up,
    local_sem,
    x_send,
    x_recv,
    c_send,
    c_recv,
    fx_send,
    fx_recv,
    fc_send,
    fc_recv,
    p_send,
    p_recv,
    r_send,
    r_recv,
):
    me = lax.axis_index("expert")
    other = {"dp": 1 - lax.axis_index("dp")}
    model_width = gx.shape[1]
    hidden_width = wg.shape[1]
    tiles = owners // tile_steps
    tile_rows = tile_steps * 2 * capacity
    f32 = jnp.float32

    def ahead(step):
        return {"expert": (me + hop_of(step, owners)) % owners}

    def behind(step):
        return {"expert": (me + owners - hop_of(step, owners)) % owners}

    def sent(ref, step):
        return ref.at[pl.ds(pl.multiple_of(step * capacity, 16), capacity), :]

    def mine(ref, step):
        return ref.at[pl.ds(pl.multiple_of(step * 2 * capacity, 16), capacity), :]

    def theirs(ref, step):
        return ref.at[pl.ds(pl.multiple_of(step * 2 * capacity + capacity, 16), capacity), :]

    def remote(src, dst, send, recv, step, device):
        return pltpu.make_async_remote_copy(
            src_ref=src,
            dst_ref=dst,
            send_sem=send.at[step],
            recv_sem=recv.at[step],
            device_id=device,
            device_id_type=MESH,
        )

    def x_copy(step):
        return remote(sent(sx, step), mine(gx, step), x_send, x_recv, step, ahead(step))

    def c_copy(step):
        return remote(sent(sc, step), mine(gc, step), c_send, c_recv, step, ahead(step))

    def fx_copy(step):
        return remote(mine(gx, step), theirs(gx, step), fx_send, fx_recv, step, other)

    def fc_copy(step):
        return remote(mine(gc, step), theirs(gc, step), fc_send, fc_recv, step, other)

    def p_copy(step):
        return remote(theirs(dx, step), sent(pin, step), p_send, p_recv, step, other)

    def r_copy(step):
        return remote(mine(dx, step), sent(ret, step), r_send, r_recv, step, behind(step))

    barrier = pltpu.get_barrier_semaphore()
    pl.semaphore_signal(barrier, inc=1, device_id=other, device_id_type=MESH)

    @pl.loop(1, owners)
    def _(hop):
        pl.semaphore_signal(
            barrier, inc=1, device_id={"expert": (me + hop) % owners}, device_id_type=MESH
        )

    pl.semaphore_wait(barrier, owners)

    def place(step):
        block = pl.ds(pl.multiple_of(step * capacity, 16), capacity)
        chosen = placing[block, :]
        sx[block, :] = jnp.dot(chosen, rows_in[...], preferred_element_type=f32).astype(jnp.bfloat16)
        placed = jnp.dot(chosen, cots_in[...], preferred_element_type=f32)
        sc[block, :] = (slot_probs[block, :] * placed).astype(jnp.bfloat16)

    @pl.loop(1, owners)
    def _(step):
        place(step)
        x_copy(step).start()
        c_copy(step).start()

    place(0)
    own = [
        pltpu.make_async_copy(sent(sx, 0), mine(gx, 0), local_sem.at[0]),
        pltpu.make_async_copy(sent(sc, 0), mine(gc, 0), local_sem.at[1]),
        pltpu.make_async_copy(w_gate, wg, local_sem.at[2]),
        pltpu.make_async_copy(w_up, wu, local_sem.at[3]),
        pltpu.make_async_copy(w_down, wd, local_sem.at[4]),
    ]
    for copy in own:
        copy.start()
    for copy in own:
        copy.wait()
    fx_copy(0).start()
    fc_copy(0).start()

    column = 256
    width = next(w for w in (512, 256, 128) if model_width % w == 0)

    @pl.loop(0, tiles)
    def _(tile):
        first = tile * tile_steps

        @pl.loop(jnp.maximum(first, 1), first + tile_steps)
        def _(step):
            x_copy(step).wait_recv()
            fx_copy(step).start()
            c_copy(step).wait_recv()
            fc_copy(step).start()

        @pl.loop(first, first + tile_steps)
        def _(step):
            fx_copy(step).wait_recv()
            fc_copy(step).wait_recv()

        rows = pl.ds(pl.multiple_of(tile * tile_rows, 16), tile_rows)

        @pl.loop(0, hidden_width // column)
        def _(part):
            cols = pl.ds(pl.multiple_of(part * column, 128), column)
            gate_pre = jnp.dot(gx[rows, :], wg[:, cols], preferred_element_type=f32)
            up_pre = jnp.dot(gx[rows, :], wu[:, cols], preferred_element_type=f32)
            d_hidden = lax.dot_general(gc[rows, :], wd[cols, :], NT, preferred_element_type=f32)
            sigmoid_gate = jax.nn.sigmoid(gate_pre)
            swish_gate = gate_pre * sigmoid_gate
            hidden[rows, cols] = (swish_gate * up_pre).astype(jnp.bfloat16)
            d_gate[rows, cols] = (
                d_hidden * up_pre * sigmoid_gate * (1.0 + gate_pre * (1.0 - sigmoid_gate))
            ).astype(jnp.bfloat16)
            d_up[rows, cols] = (d_hidden * swish_gate).astype(jnp.bfloat16)

        @pl.loop(0, model_width // width)
        def _(part):
            cols = pl.ds(pl.multiple_of(part * width, 128), width)
            total = lax.dot_general(d_gate[rows, :], wg[cols, :], NT, preferred_element_type=f32)
            total += lax.dot_general(d_up[rows, :], wu[cols, :], NT, preferred_element_type=f32)
            dx[rows, cols] = total.astype(jnp.bfloat16)

        @pl.loop(first, first + tile_steps)
        def _(step):
            p_copy(step).start()

        @pl.loop(first, first + tile_steps)
        def _(step):
            p_copy(step).wait_recv()
            held = mine(dx, step)
            held[...] = (held[...].astype(f32) + sent(pin, step)[...].astype(f32)).astype(
                jnp.bfloat16
            )

            @pl.when(step > 0)
            def _():
                r_copy(step).start()

    back = pltpu.make_async_copy(mine(dx, 0), sent(ret, 0), local_sem.at[0])
    back.start()

    @pl.loop(0, model_width // width)
    def _(part):
        cols = pl.ds(pl.multiple_of(part * width, 128), width)
        wg[cols, :] = lax.dot_general(
            gx[:, cols], d_gate[...], TN, preferred_element_type=f32
        ).astype(jnp.bfloat16)
        wu[cols, :] = lax.dot_general(
            gx[:, cols], d_up[...], TN, preferred_element_type=f32
        ).astype(jnp.bfloat16)
        wd[:, cols] = lax.dot_general(
            hidden[...], gc[:, cols], TN, preferred_element_type=f32
        ).astype(jnp.bfloat16)

    results = [
        pltpu.make_async_copy(wg, out_gate, local_sem.at[2]),
        pltpu.make_async_copy(wu, out_up, local_sem.at[3]),
        pltpu.make_async_copy(wd, out_down, local_sem.at[4]),
    ]
    for copy in results:
        copy.start()

    @pl.loop(0, owners)
    def _(step):
        fx_copy(step).wait_send()
        fc_copy(step).wait_send()
        p_copy(step).wait_send()

    @pl.loop(1, owners)
    def _(step):
        x_copy(step).wait_send()
        c_copy(step).wait_send()
        r_copy(step).wait_send()
        r_copy(step).wait_recv()

    back.wait()
    for copy in results:
        copy.wait()


def run_layer(placing, slot_probs, copy_rows, copy_cots, gate_w, up_w, down_w, owners, capacity):
    model_width = copy_rows.shape[1]
    hidden_width = gate_w.shape[1]
    slots = owners * capacity
    bf16 = jnp.bfloat16
    anywhere = pl.BlockSpec(memory_space=pl.ANY)
    tile_steps = max(1, 128 // capacity)
    return pl.pallas_call(
        functools.partial(layer_kernel, owners, capacity, tile_steps),
        out_shape=(
            jax.ShapeDtypeStruct((slots, model_width), bf16),
            jax.ShapeDtypeStruct(gate_w.shape, bf16),
            jax.ShapeDtypeStruct(up_w.shape, bf16),
            jax.ShapeDtypeStruct(down_w.shape, bf16),
        ),
        in_specs=[pl.BlockSpec(memory_space=pltpu.VMEM)] * 4 + [anywhere] * 3,
        out_specs=[anywhere] * 4,
        scratch_shapes=[
            pltpu.VMEM((slots, model_width), bf16),
            pltpu.VMEM((slots, model_width), bf16),
            pltpu.VMEM((2 * slots, model_width), bf16),
            pltpu.VMEM((2 * slots, model_width), bf16),
            pltpu.VMEM(gate_w.shape, bf16),
            pltpu.VMEM(up_w.shape, bf16),
            pltpu.VMEM(down_w.shape, bf16),
            pltpu.VMEM((2 * slots, model_width), bf16),
            pltpu.VMEM((slots, model_width), bf16),
            pltpu.VMEM((2 * slots, hidden_width), bf16),
            pltpu.VMEM((2 * slots, hidden_width), bf16),
            pltpu.VMEM((2 * slots, hidden_width), bf16),
            pltpu.SemaphoreType.DMA((5,)),
        ]
        + [pltpu.SemaphoreType.DMA((owners,))] * 12,
        compiler_params=pltpu.CompilerParams(
            collective_id=0, has_side_effects=True, vmem_limit_bytes=60 * 1024 * 1024
        ),
    )(placing, slot_probs, copy_rows, copy_cots, gate_w, up_w, down_w)


def front_rows(rows_x, rows_cot, gate_w, up_w, down_w):
    gate_pre = jnp.dot(rows_x, gate_w, preferred_element_type=jnp.float32)
    up_pre = jnp.dot(rows_x, up_w, preferred_element_type=jnp.float32)
    sigmoid_gate = jax.nn.sigmoid(gate_pre)
    swish_gate = gate_pre * sigmoid_gate
    hidden = (swish_gate * up_pre).astype(jnp.bfloat16)
    d_hidden = lax.dot_general(
        rows_cot, down_w, (((1,), (1,)), ((), ())), preferred_element_type=jnp.float32
    )
    d_gate = (d_hidden * up_pre * sigmoid_gate * (1.0 + gate_pre * (1.0 - sigmoid_gate))).astype(
        jnp.bfloat16
    )
    d_up = (d_hidden * swish_gate).astype(jnp.bfloat16)
    dx_part = lax.dot_general(
        d_gate, gate_w, (((1,), (1,)), ((), ())), preferred_element_type=jnp.float32
    )
    dx_part = dx_part + lax.dot_general(
        d_up, up_w, (((1,), (1,)), ((), ())), preferred_element_type=jnp.float32
    )
    return (hidden, d_gate, d_up, dx_part.astype(jnp.bfloat16))


def weight_sums(rows_x, rows_cot, hidden, d_gate, d_up):
    grad_gate = lax.dot_general(
        rows_x, d_gate, (((0,), (0,)), ((), ())), preferred_element_type=jnp.float32
    )
    grad_up = lax.dot_general(
        rows_x, d_up, (((0,), (0,)), ((), ())), preferred_element_type=jnp.float32
    )
    grad_down = lax.dot_general(
        hidden, rows_cot, (((0,), (0,)), ((), ())), preferred_element_type=jnp.float32
    )
    return (grad_gate, grad_up, grad_down)


def run_whole(sent_rows, sent_cots, gate_w, up_w, down_w, owners, groups, capacity):
    model_width = sent_rows.shape[1]

    def across(rows):
        blocks = rows.reshape(owners, capacity, model_width)
        came = lax.all_to_all(blocks, "expert", split_axis=0, concat_axis=0, tiled=True)
        return lax.all_gather(came, "dp", axis=0, tiled=True).reshape(-1, model_width)

    rows_x, rows_cot = across(sent_rows), across(sent_cots)
    hidden, d_gate, d_up, dx_part = front_rows(rows_x, rows_cot, gate_w, up_w, down_w)
    summed = lax.psum_scatter(
        dx_part.reshape(groups * owners, capacity, model_width),
        "dp",
        scatter_dimension=0,
        tiled=True,
    )
    returned = lax.all_to_all(summed, "expert", split_axis=0, concat_axis=0, tiled=True)
    sums = weight_sums(rows_x, rows_cot, hidden, d_gate, d_up)
    return (returned.reshape(-1, model_width), *sums)


def local(tokens, cotangent, expert_ids, gate_probs, w_gate, w_up, w_down):
    owners = lax.axis_size("expert")
    groups = lax.axis_size("dp")
    tok_rows = tokens.shape[0]
    model_width = tokens.shape[1]
    fanout = expert_ids.shape[1]
    capacity = max(2, 2 * tok_rows * fanout // owners)
    copies = tok_rows * fanout
    in_kernel = groups == 2 and capacity % 16 == 0 and owners % max(1, 128 // capacity) == 0
    flat_ids = expert_ids.reshape(copies)
    targets = jnp.arange(owners, dtype=jnp.int32)
    if in_kernel:
        targets = (lax.axis_index("expert") + hop_of(targets, owners)) % owners
    onehot = (flat_ids[:, None] == targets[None, :]).astype(jnp.int32)
    order = jnp.arange(copies, dtype=jnp.int32)
    earlier = (order[None, :] < order[:, None]).astype(jnp.float32)
    before = lax.dot(
        earlier, onehot.astype(jnp.float32), precision=lax.Precision.HIGHEST
    ).astype(jnp.int32)
    slot_rank = jnp.sum(before * onehot, axis=1)
    block = jnp.sum(onehot * jnp.arange(owners, dtype=jnp.int32)[None, :], axis=1)
    position = block * capacity + slot_rank
    copy_rows = tokens[:, None, :].reshape(copies, model_width)
    copy_tok_cot = cotangent[:, None, :].reshape(copies, model_width)
    copy_cots = (gate_probs * copy_tok_cot.astype(jnp.float32)).astype(jnp.bfloat16)
    placing = (jnp.arange(owners * capacity, dtype=jnp.int32)[:, None] == position[None, :]).astype(
        jnp.bfloat16
    )
    if in_kernel:
        probs_row = gate_probs.reshape(1, copies)
        slot_probs = jnp.sum(
            placing.astype(jnp.float32) * probs_row, axis=1, keepdims=True
        )
        returned, grad_gate, grad_up, grad_down = run_layer(
            placing, slot_probs, copy_rows, copy_tok_cot, w_gate[0], w_up[0], w_down[0], owners, capacity
        )
    else:
        sent_rows = jnp.dot(placing, copy_rows, preferred_element_type=jnp.float32).astype(jnp.bfloat16)
        sent_cots = jnp.dot(placing, copy_cots, preferred_element_type=jnp.float32).astype(jnp.bfloat16)
        returned, grad_gate, grad_up, grad_down = run_whole(
            sent_rows, sent_cots, w_gate[0], w_up[0], w_down[0], owners, groups, capacity
        )
    copy_grad = lax.dot_general(placing, returned, TN, preferred_element_type=jnp.float32)
    grad_tokens = jnp.sum(copy_grad.reshape(tok_rows, fanout, model_width), axis=1).astype(
        jnp.bfloat16
    )
    return (
        grad_tokens,
        grad_gate.astype(jnp.bfloat16)[None],
        grad_up.astype(jnp.bfloat16)[None],
        grad_down.astype(jnp.bfloat16)[None],
    )


def solution(mesh):
    return jax.shard_map(
        local,
        mesh=mesh,
        in_specs=(
            P(("dp", "expert"), None),
            P(("dp", "expert"), None),
            P(("dp", "expert"), None),
            P(("dp", "expert"), None),
            P("expert", None, "dp"),
            P("expert", None, "dp"),
            P("expert", "dp", None),
        ),
        out_specs=(
            P(("dp", "expert"), None),
            P("expert", None, "dp"),
            P("expert", None, "dp"),
            P("expert", "dp", None),
        ),
        check_vma=False,
    )
```
